256 devices in a mesh: row: 16 (over y, x_hi, core), col: 16 (over z, x_lo).
Axes of the slice: x: 4 (x_hi: 2, x_lo: 2; x = x_hi * 2 + x_lo), y: 4, z: 8, core: 2. Of those that a mesh axis runs over, the one named last changes fastest.
Arguments:
- amplitudes: bfloat16 [100, 100, 3072], P(None, None, 'col'), may hold values from -6 to 6
- integrals: bfloat16 [3072, 262144], P('col', 'row'), may hold values from -0.078125 to 0.078125
- blocks: int32 [32, 2], replicated, may hold values from 0 to 49, as said below
Outputs:
- residual: bfloat16 [128, 262144], P('col', 'row')
The draws below stay inside these ranges and needn't reach their ends.
Inputs may be any that keep to these rules, and one draw needn't show every extreme that they name: `blocks`: each row is a block pair (I, J) with I <= J, all rows distinct; the pair (0, 49) is always among them.
All inputs are finite; a program needn't handle non-finite values.
Results may differ from the reference program's by a relative error of at most 0.001.
Values may be sent and summed in bfloat16 or wider, within the bound.
No kernel may reach another device: no remote copies, remote signals or barrier semaphores. Data moves between devices by JAX's collectives and lax.ppermute only.
A program may use at most 128 MiB of HBM per device.

```python
import jax
import jax.numpy as jnp
import numpy as np
from jax import lax

OCC = 100
OB = 2
NBO = 50
K = 3072
AW = 512
NBLK = 32


def draw_blocks(key, part):
    pair_table = np.array([[upper, lower] for upper in range(NBO) for lower in range(upper, NBO)], dtype=np.int32)
    corner = NBO - 1
    count_all = pair_table.shape[0]
    ordering = np.concatenate([np.array([corner]), np.arange(corner), np.arange(corner + 1, count_all)])
    pair_table = jnp.asarray(pair_table[ordering])
    remaining = jax.random.permutation(jax.random.fold_in(key, 11), count_all - 1)[:NBLK - 1] + 1
    chosen = jnp.concatenate([jnp.zeros((1,), jnp.int32), remaining.astype(jnp.int32)])
    chosen = jax.random.permutation(jax.random.fold_in(key, 12), chosen)
    return pair_table[chosen].astype(jnp.int32)


def levels(rng, shape, pieces, least, high):
    def one(dim, shards_of):
        steps = jax.random.uniform(jax.random.fold_in(jax.random.fold_in(rng, 6), dim), (shards_of,), jnp.float32, least / len(pieces), high / len(pieces))
        return jnp.repeat(jnp.exp(steps), shape[dim] // shards_of).reshape((-1,) + (1,) * (len(shape) - dim - 1))

    level = one(*pieces[0])
    for cut in pieces[1:]:
        level = level * one(*cut)
    return level


def noise(own_key, dims, deviation, bound, split=(), kind=jnp.bfloat16):
    entries = jax.random.normal(own_key, dims, jnp.float32) * deviation
    if len(split) > 0:
        entries = levels(own_key, dims, split, -0.22, 0.18) * entries
    return jnp.clip(entries, min=-bound, max=bound).astype(kind)


def setup_inputs(seed: int = 0) -> dict:
    streams_of = jax.random.split(jax.random.key(seed), 4)
    amplitudes = noise(streams_of[0], (OCC, OCC, K), 1.0, 6.0, ((2, 16),))
    integrals = noise(streams_of[1], (K, AW * AW), (2 * K) ** -0.5, 0.078125, ((0, 16), (1, 16)))
    blocks = draw_blocks(jax.random.fold_in(streams_of[3], 71), 0)
    return dict(amplitudes=amplitudes, integrals=integrals, blocks=blocks)


def pick_rows(amplitudes, blocks):
    panel_width = amplitudes.shape[2]

    def one_block(pair_index):
        first_row = pair_index[0] * OB
        second_row = pair_index[1] * OB
        anchor = jnp.zeros((), jnp.int32)
        direct_rows = lax.dynamic_slice(amplitudes, (first_row, second_row, anchor), (OB, OB, panel_width))
        swapped_rows = lax.dynamic_slice(amplitudes, (second_row, first_row, anchor), (OB, OB, panel_width))
        return direct_rows.reshape(OB * OB, panel_width), jnp.swapaxes(swapped_rows, 0, 1).reshape(OB * OB, panel_width)

    direct_rows, swapped_rows = jax.vmap(one_block)(blocks)
    return direct_rows.reshape(-1, panel_width), swapped_rows.reshape(-1, panel_width)


def reference(amplitudes, integrals, blocks):
    forward, mirrored = pick_rows(amplitudes, blocks)
    depth = integrals.shape[0]
    flipped = jnp.swapaxes(integrals.reshape(depth, AW, AW), 1, 2).reshape(depth, AW * AW)
    total = jnp.dot(forward, integrals, preferred_element_type=jnp.float32) + jnp.dot(mirrored, flipped, preferred_element_type=jnp.float32)
    return total.astype(jnp.bfloat16)
```

```python
import functools

import jax
import jax.numpy as jnp
from jax import lax
from jax.experimental import pallas as pl
from jax.experimental.pallas import tpu as pltpu
from jax.sharding import Mesh
from jax.sharding import PartitionSpec as P

OB = 2
PB = OB * OB
A_DEV = 32
AW = 512
F32, I16 = jnp.float32, jnp.int16
ROW, Z, XL = "row", "z", "xl"
LANES = 128
TILES = A_DEV * AW // (16 * LANES)
ROW_W = TILES * LANES
TOP = 32700.0
STEPS = 256.0


def params(mib=32):
    return pltpu.CompilerParams(vmem_limit_bytes=mib << 20)


def cost(flops, bytes_accessed):
    return pl.CostEstimate(flops=flops, bytes_accessed=bytes_accessed, transcendentals=0)


def vmem():
    return pl.BlockSpec(memory_space=pltpu.VMEM)


def scale_of(tiles):
    most = functools.reduce(jnp.maximum, [jnp.abs(t) for t in tiles])
    most = jnp.max(most, axis=0, keepdims=True)
    code = jnp.ceil(jnp.log2(jnp.maximum(most, 2.0**-100)) * STEPS)
    return code, TOP * jnp.exp2(code * (-1.0 / STEPS))


def coded(x, factor):
    return jnp.round(x * factor).astype(jnp.int32).astype(I16)


def factors(codes):
    return jnp.exp2(codes.astype(F32) * (1.0 / STEPS)) * (1.0 / TOP)


def column(k, n):
    return k * ROW_W + (LANES if k >= n // 2 else 0)


def get_row(ref, start, factor):
    return [
        ref[:, start + t * LANES : start + (t + 1) * LANES].astype(jnp.int32).astype(F32) * factor
        for t in range(TILES)
    ]


def put_row(ref, start, tiles):
    code, factor = scale_of(tiles)
    for t, tile in enumerate(tiles):
        ref[:, start + t * LANES : start + (t + 1) * LANES] = coded(tile, factor)
    return code


def scale_tile(codes):
    rows = codes + [jnp.zeros((1, LANES), F32)] * (16 - len(codes))
    return jnp.concatenate(rows, axis=0).astype(jnp.int32).astype(I16)


def gather_kernel(blocks, pages, out, padded, picked):
    depth, orbitals = pages.shape[1], pages.shape[2]
    pairs = blocks.shape[0]
    lane = lax.broadcasted_iota(jnp.int32, (depth, LANES), 1)
    padded[...] = jnp.zeros_like(padded)
    picked[...] = jnp.zeros_like(picked)

    def one(pair, _):
        first, second = blocks[pair, 0] * OB, blocks[pair, 1] * OB
        base = pair * PB
        for s in range(OB):
            padded[0, :, :orbitals] = pages[first + s].astype(F32)
            padded[1, :, :orbitals] = pages[second + s].astype(F32)
            to = base + s * OB
            here = (lane >= to) & (lane < to + OB)
            picked[0] = jnp.where(here, pltpu.roll(padded[0], lax.rem(to - second + LANES, LANES), 1), picked[0])
            picked[1] = jnp.where(here, pltpu.roll(padded[1], lax.rem(to - first + LANES, LANES), 1), picked[1])
        return 0

    lax.fori_loop(0, pairs, one, 0)
    mirrored = picked[1]
    which = lax.rem(lane, PB)
    mirrored = jnp.where(
        which == 1, pltpu.roll(mirrored, LANES - 1, 1), jnp.where(which == 2, pltpu.roll(mirrored, 1, 1), mirrored)
    )
    out[0] = picked[0].T.astype(out.dtype)
    out[1] = mirrored.T.astype(out.dtype)


def gather(amplitudes, blocks):
    depth = amplitudes.shape[2]
    rows = blocks.shape[0] * PB
    return pl.pallas_call(
        gather_kernel,
        out_shape=jax.ShapeDtypeStruct((2, rows, depth), jnp.bfloat16),
        in_specs=[pl.BlockSpec(memory_space=pltpu.SMEM), vmem()],
        out_specs=vmem(),
        scratch_shapes=[pltpu.VMEM((2, depth, LANES), F32), pltpu.VMEM((2, depth, LANES), F32)],
        compiler_params=params(24),
        name="pick_rows",
    )(blocks, jnp.swapaxes(amplitudes, 1, 2))


GRID = 8


def product_kernel(z_n, n, left, right, out, whole):
    step = pl.program_id(0)
    rows = left.shape[0]
    each = A_DEV // GRID
    for i in range(each):
        part = jnp.dot(left[...], right[:, i * AW : (i + 1) * AW], preferred_element_type=F32)
        for c in range(AW // LANES):
            whole[c, pl.ds(step * each + i, rows, stride=A_DEV), :] = part[:, c * LANES : (c + 1) * LANES]

    @pl.when(step == GRID - 1)
    def _():
        def one(z, _):
            codes = []
            for k in range(n):
                tiles = [
                    whole[c, pl.ds(pl.multiple_of((z * n + k) * A_DEV + h * 16, 16), 16), :]
                    for h in range(2)
                    for c in range(AW // LANES)
                ]
                codes.append(put_row(out.at[z], column(k, n), tiles))
            out[z, :, column(n // 2, n) - LANES : column(n // 2, n)] = scale_tile(codes)
            return 0

        lax.fori_loop(0, z_n, one, 0)


def product(left, integrals, z_n):
    rows, depth = left.shape
    n = rows // z_n
    width = integrals.shape[1]
    return pl.pallas_call(
        functools.partial(product_kernel, z_n, n),
        grid=(GRID,),
        out_shape=jax.ShapeDtypeStruct((z_n, 16, n * ROW_W + LANES), I16),
        in_specs=[
            pl.BlockSpec((rows, depth), lambda s: (0, 0)),
            pl.BlockSpec((depth, width // GRID), lambda s: (0, s)),
        ],
        out_specs=pl.BlockSpec((z_n, 16, n * ROW_W + LANES), lambda s: (0, 0, 0)),
        scratch_shapes=[pltpu.VMEM((AW // LANES, rows * A_DEV, LANES), F32)],
        compiler_params=params(40),
        cost_estimate=cost(2 * rows * depth * width, 2 * depth * width + 2 * rows * width),
        name="product",
    )(left, integrals)


def step_kernel(n, first, at, got_r, got_l, own_r, own_l, out_r, out_l):
    half = n // 2
    middle = half * ROW_W
    for side, got, own, out in ((0, got_r, own_r, out_r), (1, got_l, own_l, out_l)):
        own_codes = own[0, :, middle : middle + LANES].astype(jnp.int32).astype(F32)
        own_f = factors(own_codes)
        if first:
            spot = middle if side == 0 else 0
            got_f = factors(got[:, spot : spot + LANES].astype(jnp.int32))
        else:
            got_f = factors(got[:, middle : middle + LANES].astype(jnp.int32))
        codes = []
        for k in range(n):
            start = column(k, n)
            if first and (k < half) != (side == 0):
                out[:, start : start + ROW_W] = own[0, :, start : start + ROW_W]
                codes.append(own_codes[k : k + 1])
                continue
            came = start - (middle if first and side == 1 else 0)
            a = get_row(got, came, got_f[k : k + 1])
            b = get_row(own.at[0], start, own_f[k : k + 1])
            codes.append(put_row(out, start, [x + y for x, y in zip(a, b)]))
        out[:, middle : middle + LANES] = scale_tile(codes)


def ring_step(got_r, got_l, parts, at, n, first):
    z_n, _, width = parts.shape
    shape = jax.ShapeDtypeStruct((16, width), I16)
    whole = lambda shape: pl.BlockSpec(shape, lambda s, at: (0, 0))
    return pl.pallas_call(
        functools.partial(step_kernel, n, first),
        out_shape=(shape, shape),
        grid_spec=pltpu.PrefetchScalarGridSpec(
            num_scalar_prefetch=1,
            grid=(1,),
            in_specs=[
                whole(got_r.shape),
                whole(got_l.shape),
                pl.BlockSpec((1, 16, width), lambda s, at: (at[0], 0, 0)),
                pl.BlockSpec((1, 16, width), lambda s, at: (at[1], 0, 0)),
            ],
            out_specs=[whole((16, width)), whole((16, width))],
        ),
        compiler_params=params(16),
        cost_estimate=cost(16 * width * 8, 16 * width * 12),
        name="ring_step",
    )(at, got_r, got_l, parts, parts)


def ring(parts, n):
    z_n = parts.shape[0]
    me = lax.axis_index(Z)
    right = [(i, (i + 1) % z_n) for i in range(z_n)]
    left = [((i + 1) % z_n, i) for i in range(z_n)]
    middle = n // 2 * ROW_W
    far = z_n // 2
    opposite = lax.dynamic_index_in_dim(parts, lax.rem(me + far, z_n), 0, keepdims=False)
    r, l = opposite[:, : middle + LANES], opposite[:, middle:]
    for d in range(far, 0, -1):
        r = lax.ppermute(r, Z, right)
        l = lax.ppermute(l, Z, left)
        if d > 1:
            at = jnp.stack([lax.rem(me + d - 1, z_n), lax.rem(me + z_n - d + 1, z_n)])
            r, l = ring_step(r, l, parts, at, n, d == far)
    return r, l


def end_rows(n, refs, starts_at):
    middle = n // 2 * ROW_W
    f = [factors(ref[:, middle : middle + LANES].astype(jnp.int32)) for ref in refs]

    def row(k):
        rows = [get_row(ref, column(k, n), g[k : k + 1]) for ref, g in zip(refs, f)]
        return [x + y + w for x, y, w in zip(*rows)]

    return row


def matrix(tiles):
    per = len(tiles) // 2
    return jnp.concatenate(
        [jnp.concatenate(tiles[:per], axis=1), jnp.concatenate(tiles[per:], axis=1)], axis=0
    )


def turn_kernel(n, rows_n, at, got_r, got_l, own, out):
    row = end_rows(n, [got_r, got_l, own.at[0]], None)
    groups = n // (2 * PB)
    for xl in range(2):
        codes = []
        for g in range(groups):
            stack = jnp.concatenate([matrix(row((xl * groups + g) * PB + i)) for i in range(PB)], axis=0)
            turned = stack.T
            code, factor = scale_of([turned])
            codes.append(code)
            for to in range(rows_n):
                out[to, xl, g * A_DEV : (g + 1) * A_DEV, :] = coded(turned[to * A_DEV : (to + 1) * A_DEV], factor)
        tile = scale_tile(codes)
        for to in range(rows_n):
            out[to, xl, groups * A_DEV : groups * A_DEV + 16, :] = tile


def turn(got_r, got_l, parts, n, rows_n):
    z_n, _, width = parts.shape
    whole = lambda shape: pl.BlockSpec(shape, lambda s, at: (0,) * len(shape))
    shape = (rows_n, 2, n // (2 * PB) * A_DEV + 16, LANES)
    return pl.pallas_call(
        functools.partial(turn_kernel, n, rows_n),
        out_shape=jax.ShapeDtypeStruct(shape, I16),
        grid_spec=pltpu.PrefetchScalarGridSpec(
            num_scalar_prefetch=1,
            grid=(1,),
            in_specs=[
                whole((16, width)),
                whole((16, width)),
                pl.BlockSpec((1, 16, width), lambda s, at: (at[0], 0, 0)),
            ],
            out_specs=whole(shape),
        ),
        compiler_params=params(32),
        cost_estimate=cost(16 * width * 8, 16 * width * 8),
        name="turn",
    )(lax.axis_index(Z)[None], got_r, got_l, parts)


def share_kernel(n, at, got_r, got_l, own, keep, give):
    row = end_rows(n, [got_r, got_l, own.at[0]], None)
    half = n // 2
    first = at[1] == 0
    codes = []
    for i in range(half):
        low, high = row(i), row(half + i)
        keep[i] = matrix([jnp.where(first, a, b) for a, b in zip(low, high)])
        codes.append(put_row(give, column(i, half), [jnp.where(first, b, a) for a, b in zip(low, high)]))
    give[:, column(half // 2, half) - LANES : column(half // 2, half)] = scale_tile(codes)


def share(got_r, got_l, parts, n):
    z_n, _, width = parts.shape
    half = n // 2
    whole = lambda shape: pl.BlockSpec(shape, lambda s, at: (0,) * len(shape))
    return pl.pallas_call(
        functools.partial(share_kernel, n),
        out_shape=(
            jax.ShapeDtypeStruct((half, A_DEV, AW), F32),
            jax.ShapeDtypeStruct((16, half * ROW_W + LANES), I16),
        ),
        grid_spec=pltpu.PrefetchScalarGridSpec(
            num_scalar_prefetch=1,
            grid=(1,),
            in_specs=[
                whole((16, width)),
                whole((16, width)),
                pl.BlockSpec((1, 16, width), lambda s, at: (at[0], 0, 0)),
            ],
            out_specs=[whole((half, A_DEV, AW)), whole((16, half * ROW_W + LANES))],
        ),
        compiler_params=params(16),
        cost_estimate=cost(16 * width * 8, 16 * width * 8),
        name="share",
    )(jnp.stack([lax.axis_index(Z), lax.axis_index(XL)]), got_r, got_l, parts)


def regroup(tiles):
    count = len(tiles)
    group = LANES // count
    lane = lax.broadcasted_iota(jnp.int32, tiles[0].shape, 1) // group
    out = []
    for k in range(count):
        merged = tiles[k]
        for r in range(count):
            if r != k:
                merged = jnp.where(lane == r, pltpu.roll(tiles[r], (r - k) % count * group, 1), merged)
        out.append(merged)
    return out


def last_kernel(n, rows_n, mirrored, keep, got, out, total):
    half = n // 2
    groups = half // PB
    at = groups * A_DEV
    f = [[factors(mirrored[r, s, at : at + 16, :].astype(jnp.int32)) for s in range(2)] for r in range(rows_n)]
    middle = half // 2 * ROW_W
    got_f = factors(got[:, middle : middle + LANES].astype(jnp.int32))
    for g in range(groups):
        pieces = []
        for r in range(rows_n):
            both = [
                mirrored[r, s, g * A_DEV : (g + 1) * A_DEV, :].astype(jnp.int32).astype(F32) * f[r][s][g : g + 1]
                for s in range(2)
            ]
            pieces.append(both[0] + both[1])
        per = LANES // A_DEV
        for c in range(rows_n // per):
            for i, tile in enumerate(regroup(pieces[c * per : (c + 1) * per])):
                total[c, pl.ds((g * PB + i) * A_DEV, A_DEV), :] = tile
    for k in range(half):
        tiles = get_row(got, column(k, half), got_f[k : k + 1])
        for h in range(2):
            for c in range(AW // LANES):
                lanes = slice(c * LANES, (c + 1) * LANES)
                spot = pl.ds(k * A_DEV + h * 16, 16)
                total[c, spot, :] += tiles[h * (AW // LANES) + c] + keep[k, h * 16 : (h + 1) * 16, lanes]
    for a in range(A_DEV):
        for c in range(AW // LANES):
            start = a * AW + c * LANES
            out[:, start : start + LANES] = total[c, pl.ds(a, half, stride=A_DEV), :].astype(out.dtype)


def last(mirrored, keep, got, n):
    half = n // 2
    rows_n = mirrored.shape[0]
    return pl.pallas_call(
        functools.partial(last_kernel, n, rows_n),
        out_shape=jax.ShapeDtypeStruct((half, A_DEV * AW), jnp.bfloat16),
        in_specs=[vmem()] * 3,
        out_specs=vmem(),
        scratch_shapes=[pltpu.VMEM((AW // LANES, half * A_DEV, LANES), F32)],
        compiler_params=params(16),
        name="last",
    )(mirrored, keep, got)


def on_device(rows_n, z_n, amplitudes, integrals, blocks):
    picked = gather(amplitudes, blocks)
    n = picked.shape[1] // z_n
    mirrored = product(picked[1], integrals, z_n)
    forward = product(picked[0], integrals, z_n)
    m_r, m_l = ring(mirrored, n)
    f_r, f_l = ring(forward, n)
    pieces = turn(m_r, m_l, mirrored, n, rows_n)
    shape = pieces.shape
    pieces = pieces.reshape((rows_n * 2,) + shape[2:])
    pieces = lax.all_to_all(pieces, (ROW, XL), 0, 0, tiled=True).reshape(shape)
    keep, give = share(f_r, f_l, forward, n)
    got = lax.ppermute(give, XL, [(0, 1), (1, 0)])
    return last(pieces, keep, got, n)


def solution(mesh):
    rows_n, cols_n = mesh.devices.shape
    finer = Mesh(mesh.devices.reshape(rows_n, cols_n // 2, 2), (ROW, Z, XL))
    return jax.shard_map(
        functools.partial(on_device, rows_n, cols_n // 2),
        mesh=finer,
        in_specs=(P(None, None, (Z, XL)), P((Z, XL), ROW), P()),
        out_specs=P((Z, XL), ROW),
        check_vma=False,
    )
```

```python
import functools

import jax
import jax.numpy as jnp
from jax import lax
from jax.experimental import pallas as pl
from jax.experimental.pallas import tpu as pltpu
from jax.sharding import Mesh
from jax.sharding import PartitionSpec as P

OB = 2
PB = OB * OB
A_DEV = 32
AW = 512
F32, I16 = jnp.float32, jnp.int16
ROW, Z, XL = "row", "z", "xl"
LANES = 128
TILES = A_DEV * AW // (16 * LANES)
ROW_W = TILES * LANES
PITCH = A_DEV + 1
PARTS = 1
TOP = 32700.0
STEPS = 256.0


def params(mib=32):
    return pltpu.CompilerParams(vmem_limit_bytes=mib << 20)


def cost(flops, bytes_accessed):
    return pl.CostEstimate(flops=flops, bytes_accessed=bytes_accessed, transcendentals=0)


def hbm():
    return pl.BlockSpec(memory_space=pltpu.HBM)


def vmem():
    return pl.BlockSpec(memory_space=pltpu.VMEM)


def scale_of(tiles):
    most = functools.reduce(jnp.maximum, [jnp.abs(t) for t in tiles])
    most = jnp.max(most, axis=0, keepdims=True)
    code = jnp.ceil(jnp.log2(jnp.maximum(most, 2.0**-100)) * STEPS)
    return code, TOP * jnp.exp2(code * (-1.0 / STEPS))


def coded(x, factor):
    return jnp.round(x * factor).astype(jnp.int32).astype(I16)


def factors(codes):
    return jnp.exp2(codes.astype(F32) * (1.0 / STEPS)) * (1.0 / TOP)


def column(k, n):
    return k * ROW_W + (LANES if k >= n // 2 else 0)


def get_row(ref, start, factor):
    return [
        ref[:, start + t * LANES : start + (t + 1) * LANES].astype(jnp.int32).astype(F32) * factor
        for t in range(TILES)
    ]


def put_row(ref, start, tiles):
    code, factor = scale_of(tiles)
    for t, tile in enumerate(tiles):
        ref[:, start + t * LANES : start + (t + 1) * LANES] = coded(tile, factor)
    return code


def scale_tile(codes):
    rows = codes + [jnp.zeros((1, LANES), F32)] * (16 - len(codes))
    return jnp.concatenate(rows, axis=0).astype(jnp.int32).astype(I16)


UNROLL = 4


def gather_kernel(blocks, pages, out, picked):
    depth, orbitals = pages.shape[1], pages.shape[2]
    pairs = blocks.shape[1]
    lane = lax.broadcasted_iota(jnp.int32, (depth, LANES), 1)
    blank = jnp.zeros((depth, LANES - orbitals), F32)
    picked[...] = jnp.zeros_like(picked)

    def turned(page, shift):
        whole = jnp.concatenate([pages[page].astype(F32), blank], axis=1)
        return pltpu.roll(whole, lax.rem(shift + LANES, LANES), 1)

    def some(step, _):
        forward, mirrored = picked[0], picked[1]
        for i in range(UNROLL):
            pair = step * UNROLL + i
            first, second = blocks[0, pair] * OB, blocks[1, pair] * OB
            for s in range(OB):
                to = pair * PB + s * OB
                here = (lane >= to) & (lane < to + OB)
                forward = jnp.where(here, turned(first + s, to - second), forward)
                mirrored = jnp.where(here, turned(second + s, to - first), mirrored)
        picked[0] = forward
        picked[1] = mirrored
        return 0

    lax.fori_loop(0, pairs // UNROLL, some, 0)
    mirrored = picked[1]
    which = lax.rem(lane, PB)
    mirrored = jnp.where(
        which == 1, pltpu.roll(mirrored, LANES - 1, 1), jnp.where(which == 2, pltpu.roll(mirrored, 1, 1), mirrored)
    )
    out[:LANES] = mirrored.T.astype(out.dtype)
    out[LANES:] = picked[0].T.astype(out.dtype)


def gather(amplitudes, blocks):
    depth = amplitudes.shape[2]
    rows = blocks.shape[0] * PB
    return pl.pallas_call(
        gather_kernel,
        out_shape=jax.ShapeDtypeStruct((2 * rows, depth), jnp.bfloat16),
        in_specs=[pl.BlockSpec(memory_space=pltpu.SMEM), vmem()],
        out_specs=vmem(),
        scratch_shapes=[pltpu.VMEM((2, depth, LANES), F32)],
        compiler_params=params(24),
        name="pick_rows",
    )(blocks.T, jnp.swapaxes(amplitudes, 1, 2))


GRID = 8


def fill(left, right, whole):
    step = pl.program_id(0)
    rows = left.shape[0]
    each = A_DEV // GRID
    for i in range(each):
        part = jnp.dot(left[...], right[:, i * AW : (i + 1) * AW], preferred_element_type=F32)
        for c in range(AW // LANES):
            whole[c, pl.ds(step * each + i, rows, stride=PITCH), :] = part[:, c * LANES : (c + 1) * LANES]


def filled(whole, row):
    return [
        whole[c, pl.ds(row * PITCH + h * 16, 16), :] for h in range(2) for c in range(AW // LANES)
    ]


def product_kernel(z_n, n, at, left, right, *refs):
    *outs, out_r, out_l, whole, coded_rows, sems = refs
    fill(left, right, whole)

    @pl.when(pl.program_id(0) == GRID - 1)
    def _():
        middle = n // 2 * ROW_W
        for kind in range(2):
            out = outs[kind]
            base = kind * z_n

            def one(z, _):
                spot = coded_rows.at[base + z]
                codes = [put_row(spot, column(k, n), filled(whole, (base + z) * n + k)) for k in range(n)]
                spot[:, middle : middle + LANES] = scale_tile(codes)
                pltpu.make_async_copy(spot, out.at[z], sems.at[base + z]).start()
                return 0

            lax.fori_loop(0, z_n, one, 0)
            opposite = coded_rows.at[base + at[0]]
            out_r[kind] = opposite[:, : middle + LANES]
            out_l[kind] = opposite[:, middle:]
        for kind in range(2):
            for z in range(z_n):
                spot = kind * z_n + z
                pltpu.make_async_copy(coded_rows.at[spot], outs[kind].at[z], sems.at[spot]).wait()


def product(left, integrals, z_n):
    depth, width = integrals.shape
    rows = left.shape[0]
    n = rows // 2 // z_n
    total = n * ROW_W + LANES
    half = n // 2 * ROW_W + LANES
    at = lax.rem(lax.axis_index(Z) + z_n // 2, z_n)[None]
    end = jax.ShapeDtypeStruct((2, 16, half), I16)
    end_spec = pl.BlockSpec((2, 16, half), lambda s: (0, 0, 0))
    *parts, r, l = pl.pallas_call(
        functools.partial(product_kernel, z_n, n),
        grid=(GRID,),
        out_shape=(pltpu.HBM((z_n, 16, total), I16),) * 2 + (end, end),
        in_specs=[
            smem(),
            pl.BlockSpec((rows, depth), lambda s: (0, 0)),
            pl.BlockSpec((depth, width // GRID), lambda s: (0, s)),
        ],
        out_specs=[hbm(), hbm(), end_spec, end_spec],
        scratch_shapes=[
            pltpu.VMEM(matrices(rows), F32),
            pltpu.VMEM((2 * z_n, 16, total), I16),
            pltpu.SemaphoreType.DMA((2 * z_n,)),
        ],
        compiler_params=params(PRODUCT_MIB),
        cost_estimate=cost(2 * rows * depth * width, 2 * depth * width + 2 * rows * width),
        name="product",
    )(at, left, in_hbm(integrals))
    return parts, r, l


def in_hbm(x):
    return pltpu.with_memory_space_constraint(x, pltpu.HBM)


PRODUCT_MIB = 48


def matrices(rows):
    return (AW // LANES, rows * PITCH, LANES)


def step_kernel(n, kind, first, at, got_r, got_l, parts, after, out_r, out_l, own_r, own_l, sems):
    half = n // 2
    middle = half * ROW_W
    if first:
        got_r, got_l = got_r.at[kind], got_l.at[kind]
    copies = [
        pltpu.make_async_copy(parts.at[at[i]], own, sems.at[i]) for i, own in enumerate((own_r, own_l))
    ]
    for copy in copies:
        copy.start()
    for side, got, own, out in ((0, got_r, own_r, out_r), (1, got_l, own_l, out_l)):
        copies[side].wait()
        own_codes = own[:, middle : middle + LANES].astype(jnp.int32).astype(F32)
        own_f = factors(own_codes)
        if first:
            spot = middle if side == 0 else 0
            got_f = factors(got[:, spot : spot + LANES].astype(jnp.int32))
        else:
            got_f = factors(got[:, middle : middle + LANES].astype(jnp.int32))
        codes = []
        for k in range(n):
            start = column(k, n)
            if first and (k < half) != (side == 0):
                out[:, start : start + ROW_W] = own[:, start : start + ROW_W]
                codes.append(own_codes[k : k + 1])
                continue
            came = start - (middle if first and side == 1 else 0)
            a = get_row(got, came, got_f[k : k + 1])
            b = get_row(own, start, own_f[k : k + 1])
            codes.append(put_row(out, start, [x + y for x, y in zip(a, b)]))
        out[:, middle : middle + LANES] = scale_tile(codes)


def smem():
    return pl.BlockSpec(memory_space=pltpu.SMEM)


def anywhere():
    return pl.BlockSpec(memory_space=pl.ANY)


def ring_step(got_r, got_l, parts, at, n, kind, first, after):
    width = parts.shape[2]
    shape = jax.ShapeDtypeStruct((16, width), I16)
    return pl.pallas_call(
        functools.partial(step_kernel, n, kind, first),
        out_shape=(shape, shape),
        in_specs=[smem(), vmem(), vmem(), hbm(), anywhere()],
        out_specs=[vmem(), vmem()],
        scratch_shapes=[pltpu.VMEM((16, width), I16), pltpu.VMEM((16, width), I16), pltpu.SemaphoreType.DMA((2,))],
        compiler_params=params(16),
        cost_estimate=cost(16 * width * 8, 16 * width * 12),
        name="ring_step",
    )(at, got_r, got_l, in_hbm(parts), after)


def rings(streams, r, l, n, z_n):
    me = lax.axis_index(Z)
    right = [(i, (i + 1) % z_n) for i in range(z_n)]
    left = [((i + 1) % z_n, i) for i in range(z_n)]
    far = z_n // 2
    sums = [(lax.ppermute(r, Z, right), lax.ppermute(l, Z, left))] * len(streams)
    for d in range(far - 1, 0, -1):
        at = jnp.stack([lax.rem(me + d, z_n), lax.rem(me + z_n - d, z_n)])
        after = at
        for i, (parts, (r, l)) in enumerate(zip(streams, sums)):
            sums[i] = ring_step(r, l, parts, at, n, i, d == far - 1, after)
            after = sums[i][0]
        sums = [(lax.ppermute(r, Z, right), lax.ppermute(l, Z, left)) for r, l in sums]
    return sums


def end_rows(n, refs):
    middle = n // 2 * ROW_W
    f = [factors(ref[:, middle : middle + LANES].astype(jnp.int32)) for ref in refs]

    def row(k):
        rows = [get_row(ref, column(k, n), g[k : k + 1]) for ref, g in zip(refs, f)]
        return [x + y + w for x, y, w in zip(*rows)]

    return row


def matrix(tiles):
    per = len(tiles) // 2
    return jnp.concatenate(
        [jnp.concatenate(tiles[:per], axis=1), jnp.concatenate(tiles[per:], axis=1)], axis=0
    )


def fetch(parts, at, own, sem):
    copy = pltpu.make_async_copy(parts.at[at], own, sem)
    copy.start()
    copy.wait()


def turn_kernel(n, rows_n, at, got_r, got_l, parts, out, own, sem):
    fetch(parts, at[0], own, sem)
    row = end_rows(n, [got_r, got_l, own])
    groups = n // (2 * PB)
    for xl in range(2):
        codes = []
        for g in range(groups):
            stack = jnp.concatenate([matrix(row((xl * groups + g) * PB + i)) for i in range(PB)], axis=0)
            turned = stack.T
            code, factor = scale_of([turned])
            codes.append(code)
            for to in range(rows_n):
                out[to, xl, g * A_DEV : (g + 1) * A_DEV, :] = coded(turned[to * A_DEV : (to + 1) * A_DEV], factor)
        tile = scale_tile(codes)
        for to in range(rows_n):
            out[to, xl, groups * A_DEV : groups * A_DEV + 16, :] = tile


def turn(got_r, got_l, parts, n, rows_n):
    width = parts.shape[2]
    shape = (rows_n, 2, n // (2 * PB) * A_DEV + 16, LANES)
    return pl.pallas_call(
        functools.partial(turn_kernel, n, rows_n),
        out_shape=jax.ShapeDtypeStruct(shape, I16),
        in_specs=[smem(), vmem(), vmem(), hbm()],
        out_specs=vmem(),
        scratch_shapes=[pltpu.VMEM((16, width), I16), pltpu.SemaphoreType.DMA],
        compiler_params=params(32),
        cost_estimate=cost(16 * width * 8, 16 * width * 8),
        name="turn",
    )(lax.axis_index(Z)[None], got_r, got_l, in_hbm(parts))


def share_kernel(n, at, got_r, got_l, parts, keep, give, own, sem):
    fetch(parts, at[0], own, sem)
    row = end_rows(n, [got_r, got_l, own])
    half = n // 2
    first = at[1] == 0
    codes = []
    for i in range(half):
        low, high = row(i), row(half + i)
        keep[i] = matrix([jnp.where(first, a, b) for a, b in zip(low, high)])
        codes.append(put_row(give, column(i, half), [jnp.where(first, b, a) for a, b in zip(low, high)]))
    give[:, column(half // 2, half) - LANES : column(half // 2, half)] = scale_tile(codes)


def share(got_r, got_l, parts, n):
    width = parts.shape[2]
    half = n // 2
    return pl.pallas_call(
        functools.partial(share_kernel, n),
        out_shape=(
            jax.ShapeDtypeStruct((half, A_DEV, AW), F32),
            jax.ShapeDtypeStruct((16, half * ROW_W + LANES), I16),
        ),
        in_specs=[smem(), vmem(), vmem(), hbm()],
        out_specs=[vmem(), vmem()],
        scratch_shapes=[pltpu.VMEM((16, width), I16), pltpu.SemaphoreType.DMA],
        compiler_params=params(16),
        cost_estimate=cost(16 * width * 8, 16 * width * 8),
        name="share",
    )(jnp.stack([lax.axis_index(Z), lax.axis_index(XL)]), got_r, got_l, in_hbm(parts))


def regroup(tiles):
    count = len(tiles)
    group = LANES // count
    lane = lax.broadcasted_iota(jnp.int32, tiles[0].shape, 1) // group
    out = []
    for k in range(count):
        merged = tiles[k]
        for r in range(count):
            if r != k:
                merged = jnp.where(lane == r, pltpu.roll(tiles[r], (r - k) % count * group, 1), merged)
        out.append(merged)
    return out


def last_kernel(n, rows_n, mirrored, keep_0, got_0, out, total):
    half = n // 2
    groups = half // PB
    at = groups * A_DEV
    f = [[factors(mirrored[r, s, at : at + 16, :].astype(jnp.int32)) for s in range(2)] for r in range(rows_n)]
    middle = half // 2 * ROW_W
    for g in range(groups):
        pieces = []
        for r in range(rows_n):
            both = [
                mirrored[r, s, g * A_DEV : (g + 1) * A_DEV, :].astype(jnp.int32).astype(F32) * f[r][s][g : g + 1]
                for s in range(2)
            ]
            pieces.append(both[0] + both[1])
        per = LANES // A_DEV
        for c in range(rows_n // per):
            for i, tile in enumerate(regroup(pieces[c * per : (c + 1) * per])):
                total[c, pl.ds((g * PB + i) * PITCH, A_DEV), :] = tile
    for part, keep, got in ((0, keep_0, got_0),):
        got_f = factors(got[:, middle : middle + LANES].astype(jnp.int32))
        for k in range(half):
            tiles = get_row(got, column(k, half), got_f[k : k + 1])
            for h in range(2):
                for c in range(AW // LANES):
                    lanes = slice(c * LANES, (c + 1) * LANES)
                    spot = pl.ds((part * half + k) * PITCH + h * 16, 16)
                    tile = tiles[h * (AW // LANES) + c] + keep[k, h * 16 : (h + 1) * 16, lanes]
                    total[c, spot, :] = tile + total[c, spot, :] if part == 0 else tile
    for a in range(A_DEV):
        for c in range(AW // LANES):
            start = a * AW + c * LANES
            out[:, start : start + LANES] = total[c, pl.ds(a, PARTS * half, stride=PITCH), :].astype(out.dtype)


def last(mirrored, shares, n):
    rows = PARTS * n // 2
    rows_n = mirrored.shape[0]
    return pl.pallas_call(
        functools.partial(last_kernel, n, rows_n),
        out_shape=jax.ShapeDtypeStruct((rows, A_DEV * AW), jnp.bfloat16),
        in_specs=[vmem()] * 3,
        out_specs=vmem(),
        scratch_shapes=[pltpu.VMEM(matrices(rows), F32)],
        compiler_params=params(16),
        name="last",
    )(mirrored, *shares)


def swap(keep, give):
    return keep, lax.ppermute(give, XL, [(0, 1), (1, 0)])


def on_device(rows_n, z_n, amplitudes, integrals, blocks):
    picked = gather(amplitudes, blocks)
    rows = picked.shape[0] // 2
    n = rows // z_n
    streams, r, l = product(picked, integrals, z_n)
    (m_r, m_l), (f_r, f_l) = rings(streams, r, l, n, z_n)
    pieces = turn(m_r, m_l, streams[0], n, rows_n)
    shape = pieces.shape
    pieces = pieces.reshape((rows_n * 2,) + shape[2:])
    pieces = lax.all_to_all(pieces, (ROW, XL), 0, 0, tiled=True).reshape(shape)
    keep, got = swap(*share(f_r, f_l, streams[1], n))
    return last(pieces, (keep, got), n)


def solution(mesh):
    rows_n, cols_n = mesh.devices.shape
    finer = Mesh(mesh.devices.reshape(rows_n, cols_n // 2, 2), (ROW, Z, XL))
    return jax.shard_map(
        functools.partial(on_device, rows_n, cols_n // 2),
        mesh=finer,
        in_specs=(P(None, None, (Z, XL)), P((Z, XL), ROW), P()),
        out_specs=P((Z, XL), ROW),
        check_vma=False,
    )
```

```python
import functools

import jax
import jax.numpy as jnp
from jax import lax
from jax.experimental import pallas as pl
from jax.experimental.pallas import tpu as pltpu
from jax.sharding import Mesh
from jax.sharding import PartitionSpec as P

OB = 2
PB = OB * OB
A_DEV = 32
AW = 512
F32, I16 = jnp.float32, jnp.int16
ROW, Z, XL = "row", "z", "xl"
LANES = 128
TILES = A_DEV * AW // (16 * LANES)
ROW_W = TILES * LANES
PITCH = A_DEV + 1
TOP = 32700.0
STEPS = 256.0


def params(mib=32):
    return pltpu.CompilerParams(vmem_limit_bytes=mib << 20)


def cost(flops, bytes_accessed):
    return pl.CostEstimate(flops=flops, bytes_accessed=bytes_accessed, transcendentals=0)


def hbm():
    return pl.BlockSpec(memory_space=pltpu.HBM)


def vmem():
    return pl.BlockSpec(memory_space=pltpu.VMEM)


def scale_of(tiles):
    most = functools.reduce(jnp.maximum, [jnp.abs(t) for t in tiles])
    most = jnp.max(most, axis=0, keepdims=True)
    code = jnp.ceil(jnp.log2(jnp.maximum(most, 2.0**-100)) * STEPS)
    return code, TOP * jnp.exp2(code * (-1.0 / STEPS))


def coded(x, factor):
    return jnp.round(x * factor).astype(jnp.int32).astype(I16)


def factors(codes):
    return jnp.exp2(codes.astype(F32) * (1.0 / STEPS)) * (1.0 / TOP)


def column(k, n):
    return k * ROW_W + (LANES if k >= n // 2 else 0)


def get_row(ref, start, factor):
    return [
        ref[:, start + t * LANES : start + (t + 1) * LANES].astype(jnp.int32).astype(F32) * factor
        for t in range(TILES)
    ]


def put_row(ref, start, tiles):
    code, factor = scale_of(tiles)
    for t, tile in enumerate(tiles):
        ref[:, start + t * LANES : start + (t + 1) * LANES] = coded(tile, factor)
    return code


def scale_tile(codes):
    rows = codes + [jnp.zeros((1, LANES), F32)] * (16 - len(codes))
    return jnp.concatenate(rows, axis=0).astype(jnp.int32).astype(I16)


UNROLL = 4


def gather_kernel(z_n, at, blocks, pages, out, picked):
    depth, orbitals = pages.shape[1], pages.shape[2]
    pairs = blocks.shape[1]
    each = pairs // (2 * z_n)
    lane = lax.broadcasted_iota(jnp.int32, (depth, LANES), 1)
    blank = jnp.zeros((depth, LANES - orbitals), F32)
    picked[...] = jnp.zeros_like(picked)

    def turned(page, shift):
        whole = jnp.concatenate([pages[page].astype(F32), blank], axis=1)
        return pltpu.roll(whole, lax.rem(shift + LANES, LANES), 1)

    def some(step, _):
        forward, mirrored = picked[0], picked[1]
        for i in range(UNROLL):
            pair = step * UNROLL + i
            first, second = blocks[0, pair] * OB, blocks[1, pair] * OB
            device, g = pair // each, lax.rem(pair, each)
            z, other = device // 2, lax.rem(device + at[0], 2)
            base_f = (other * z_n + z) * each * PB + g * PB
            for s in range(OB):
                to = base_f + s * OB
                here = (lane >= to) & (lane < to + OB)
                forward = jnp.where(here, turned(first + s, to - second), forward)
                to = pair * PB + s * OB
                here = (lane >= to) & (lane < to + OB)
                mirrored = jnp.where(here, turned(second + s, to - first), mirrored)
        picked[0] = forward
        picked[1] = mirrored
        return 0

    lax.fori_loop(0, pairs // UNROLL, some, 0)
    mirrored = picked[1]
    which = lax.rem(lane, PB)
    mirrored = jnp.where(
        which == 1, pltpu.roll(mirrored, LANES - 1, 1), jnp.where(which == 2, pltpu.roll(mirrored, 1, 1), mirrored)
    )
    out[:LANES] = mirrored.T.astype(out.dtype)
    out[LANES:] = picked[0].T.astype(out.dtype)


def gather(amplitudes, blocks, z_n):
    depth = amplitudes.shape[2]
    rows = blocks.shape[0] * PB
    return pl.pallas_call(
        functools.partial(gather_kernel, z_n),
        out_shape=jax.ShapeDtypeStruct((2 * rows, depth), jnp.bfloat16),
        in_specs=[smem(), smem(), vmem()],
        out_specs=vmem(),
        scratch_shapes=[pltpu.VMEM((2, depth, LANES), F32)],
        compiler_params=params(24),
        name="pick_rows",
    )(lax.axis_index(XL)[None], blocks.T, jnp.swapaxes(amplitudes, 1, 2))


GRID = 8


def fill(left, right, whole):
    step = pl.program_id(0)
    rows = left.shape[0]
    each = A_DEV // GRID
    for i in range(each):
        part = jnp.dot(left[...], right[:, i * AW : (i + 1) * AW], preferred_element_type=F32)
        for c in range(AW // LANES):
            whole[c, pl.ds(step * each + i, rows, stride=PITCH), :] = part[:, c * LANES : (c + 1) * LANES]


def filled(whole, row):
    return [
        whole[c, pl.ds(row * PITCH + h * 16, 16), :] for h in range(2) for c in range(AW // LANES)
    ]


def product_kernel(segments, at, left, right, *refs):
    count = len(segments)
    parts, (out_r, out_l, whole) = refs[:count], refs[count : count + 3]
    coded_rows, sems = refs[count + 3 : 2 * count + 3], refs[-1]
    fill(left, right, whole)

    @pl.when(pl.program_id(0) == GRID - 1)
    def _():
        z_n = parts[0].shape[0]
        first_row = 0
        for i, n in enumerate(segments):
            middle = n // 2 * ROW_W

            def one(z, _, i=i, n=n, first_row=first_row, middle=middle):
                spot = coded_rows[i].at[z]
                codes = [put_row(spot, column(k, n), filled(whole, first_row + z * n + k)) for k in range(n)]
                spot[:, middle : middle + LANES] = scale_tile(codes)
                pltpu.make_async_copy(spot, parts[i].at[z], sems.at[i, z]).start()
                return 0

            lax.fori_loop(0, z_n, one, 0)
            if i == 0:
                opposite = coded_rows[0].at[at[0]]
                out_r[...] = opposite[:, : middle + LANES]
                out_l[...] = opposite[:, middle:]
            first_row += z_n * n
        for i in range(count):
            for z in range(z_n):
                pltpu.make_async_copy(coded_rows[i].at[z], parts[i].at[z], sems.at[i, z]).wait()


def far_side(z_n):
    return lax.rem(lax.axis_index(Z) + z_n // 2, z_n)[None]


def product(left, integrals, z_n, segments):
    rows, depth = left.shape
    width = integrals.shape[1]
    end = jax.ShapeDtypeStruct((16, segments[0] // 2 * ROW_W + LANES), I16)
    shapes = [(z_n, 16, n * ROW_W + LANES) for n in segments]
    return pl.pallas_call(
        functools.partial(product_kernel, segments),
        grid=(GRID,),
        out_shape=[pltpu.HBM(shape, I16) for shape in shapes] + [end, end],
        in_specs=[
            smem(),
            pl.BlockSpec((rows, depth), lambda s: (0, 0)),
            pl.BlockSpec((depth, width // GRID), lambda s: (0, s)),
        ],
        out_specs=[hbm() for _ in shapes] + [pl.BlockSpec(end.shape, lambda s: (0, 0))] * 2,
        scratch_shapes=[pltpu.VMEM(matrices(rows), F32)]
        + [pltpu.VMEM(shape, I16) for shape in shapes]
        + [pltpu.SemaphoreType.DMA((len(segments), z_n))],
        compiler_params=params(48),
        cost_estimate=cost(2 * rows * depth * width, 2 * depth * width + 2 * rows * width),
        name="product",
    )(far_side(z_n), left, in_hbm(integrals))


def in_hbm(x):
    return pltpu.with_memory_space_constraint(x, pltpu.HBM)


def matrices(rows):
    return (AW // LANES, rows * PITCH, LANES)


def smem():
    return pl.BlockSpec(memory_space=pltpu.SMEM)


def anywhere():
    return pl.BlockSpec(memory_space=pl.ANY)


def scales(ref, n):
    middle = n // 2 * ROW_W
    return factors(ref[:, middle : middle + LANES].astype(jnp.int32))


def total_row(refs, scale, k, n):
    rows = [get_row(ref, column(k, n), f[k : k + 1]) for ref, f in zip(refs, scale)]
    return [functools.reduce(jnp.add, tiles) for tiles in zip(*rows)]


def fetch(parts, at, own, sems):
    copies = [pltpu.make_async_copy(part.at[at], own.at[i], sems.at[i]) for i, part in enumerate(parts)]
    for copy in copies:
        copy.start()

    def wait():
        for copy in copies:
            copy.wait()

    return wait


def own_scratch(parts):
    return [pltpu.VMEM((len(parts),) + parts[0].shape[1:], I16), pltpu.SemaphoreType.DMA((len(parts),))]


def open_kernel(n, at, *refs):
    *parts, out_r, out_l, own, sems = refs
    fetch(parts, at[0], own, sems)()
    terms = [own.at[i] for i in range(len(parts))]
    f = [scales(ref, n) for ref in terms]
    half = n // 2
    for out, rows in ((out_r, range(half)), (out_l, range(half, n))):
        start = 0 if out is out_r else LANES
        codes = [jnp.zeros((1, LANES), F32)] * rows[0]
        for i, k in enumerate(rows):
            codes.append(put_row(out, start + i * ROW_W, total_row(terms, f, k, n)))
        spot = half * ROW_W if out is out_r else 0
        out[:, spot : spot + LANES] = scale_tile(codes)


def open_ring(parts, n):
    z_n = parts[0].shape[0]
    end = jax.ShapeDtypeStruct((16, n // 2 * ROW_W + LANES), I16)
    return pl.pallas_call(
        functools.partial(open_kernel, n),
        out_shape=[end, end],
        in_specs=[smem()] + [hbm() for _ in parts],
        out_specs=[vmem(), vmem()],
        scratch_shapes=own_scratch(parts),
        compiler_params=params(16),
        cost_estimate=cost(1000, 3000000),
        name="open_ring",
    )(far_side(z_n), *map(in_hbm, parts))


def step_kernel(n, side, first, at, got, *refs):
    *parts, _, out, own, sems = refs
    half = n // 2
    middle = half * ROW_W
    wait = fetch(parts, at[0], own, sems)
    spot = (middle if side == 0 else 0) if first else middle
    got_f = factors(got[:, spot : spot + LANES].astype(jnp.int32))
    wait()
    terms = [own.at[i] for i in range(len(parts))]
    f = [scales(ref, n) for ref in terms]
    codes = []
    for k in range(n):
        start = column(k, n)
        tiles = total_row(terms, f, k, n)
        if not first or (k < half) == (side == 0):
            came = get_row(got, start - (middle if first and side == 1 else 0), got_f[k : k + 1])
            tiles = [a + b for a, b in zip(tiles, came)]
        codes.append(put_row(out, start, tiles))
    out[:, middle : middle + LANES] = scale_tile(codes)


def ring_step(got, parts, at, n, side, first, after):
    width = parts[0].shape[2]
    return pl.pallas_call(
        functools.partial(step_kernel, n, side, first),
        out_shape=jax.ShapeDtypeStruct((16, width), I16),
        in_specs=[smem(), vmem()] + [hbm() for _ in parts] + [anywhere()],
        out_specs=vmem(),
        scratch_shapes=own_scratch(parts),
        compiler_params=params(16),
        cost_estimate=cost(1000, 3000000),
        name="ring_step",
    )(at, got, *map(in_hbm, parts), after)


def ring(parts, r, l, n):
    z_n = parts[0].shape[0]
    me = lax.axis_index(Z)
    right = [(i, (i + 1) % z_n) for i in range(z_n)]
    left = [((i + 1) % z_n, i) for i in range(z_n)]
    far = z_n // 2
    r, l = lax.ppermute(r, Z, right), lax.ppermute(l, Z, left)
    for d in range(far - 1, 0, -1):
        first = d == far - 1
        at = lax.rem(me + d, z_n)[None]
        r = ring_step(r, parts, at, n, 0, first, at)
        l = ring_step(l, parts, lax.rem(me + z_n - d, z_n)[None], n, 1, first, r)
        r, l = lax.ppermute(r, Z, right), lax.ppermute(l, Z, left)
    return r, l


def matrix(tiles):
    per = len(tiles) // 2
    return jnp.concatenate(
        [jnp.concatenate(tiles[:per], axis=1), jnp.concatenate(tiles[per:], axis=1)], axis=0
    )


def turn_kernel(n, rows_n, at, got_r, got_l, parts, out, own, sems):
    fetch([parts], at[0], own, sems)()
    terms = [got_r, got_l, own.at[0]]
    f = [scales(ref, n) for ref in terms]
    groups = n // (2 * PB)
    for xl in range(2):
        codes = []
        for g in range(groups):
            stack = jnp.concatenate([matrix(total_row(terms, f, (xl * groups + g) * PB + i, n)) for i in range(PB)], axis=0)
            turned = stack.T
            code, factor = scale_of([turned])
            codes.append(code)
            for to in range(rows_n):
                out[to, xl, g * A_DEV : (g + 1) * A_DEV, :] = coded(turned[to * A_DEV : (to + 1) * A_DEV], factor)
        tile = scale_tile(codes)
        for to in range(rows_n):
            out[to, xl, groups * A_DEV : groups * A_DEV + 16, :] = tile


def turn(got_r, got_l, parts, n, rows_n):
    width = parts.shape[2]
    shape = (rows_n, 2, n // (2 * PB) * A_DEV + 16, LANES)
    return pl.pallas_call(
        functools.partial(turn_kernel, n, rows_n),
        out_shape=jax.ShapeDtypeStruct(shape, I16),
        in_specs=[smem(), vmem(), vmem(), hbm()],
        out_specs=vmem(),
        scratch_shapes=own_scratch([parts]),
        compiler_params=params(32),
        cost_estimate=cost(16 * width * 8, 16 * width * 8),
        name="turn",
    )(lax.axis_index(Z)[None], got_r, got_l, in_hbm(parts))


def regroup(tiles):
    count = len(tiles)
    group = LANES // count
    lane = lax.broadcasted_iota(jnp.int32, tiles[0].shape, 1) // group
    out = []
    for k in range(count):
        merged = tiles[k]
        for r in range(count):
            if r != k:
                merged = jnp.where(lane == r, pltpu.roll(tiles[r], (r - k) % count * group, 1), merged)
        out.append(merged)
    return out


def last_kernel(n, rows_n, at, mirrored, r, l, *refs):
    *parts, out, total, own, sems = refs
    wait = fetch(parts, at[0], own, sems)
    groups = n // PB
    spot = groups * A_DEV
    f = [[factors(mirrored[row, s, spot : spot + 16, :].astype(jnp.int32)) for s in range(2)] for row in range(rows_n)]
    for g in range(groups):
        pieces = []
        for row in range(rows_n):
            both = [
                mirrored[row, s, g * A_DEV : (g + 1) * A_DEV, :].astype(jnp.int32).astype(F32) * f[row][s][g : g + 1]
                for s in range(2)
            ]
            pieces.append(both[0] + both[1])
        per = LANES // A_DEV
        for c in range(rows_n // per):
            for i, tile in enumerate(regroup(pieces[c * per : (c + 1) * per])):
                total[c, pl.ds((g * PB + i) * PITCH, A_DEV), :] = tile
    wait()
    terms = [r, l] + [own.at[i] for i in range(len(parts))]
    scale = [scales(ref, n) for ref in terms]
    for k in range(n):
        tiles = total_row(terms, scale, k, n)
        for h in range(2):
            for c in range(AW // LANES):
                total[c, pl.ds(k * PITCH + h * 16, 16), :] += tiles[h * (AW // LANES) + c]
    for a in range(A_DEV):
        for c in range(AW // LANES):
            start = a * AW + c * LANES
            out[:, start : start + LANES] = total[c, pl.ds(a, n, stride=PITCH), :].astype(out.dtype)


def last(mirrored, r, l, parts, n):
    rows_n = mirrored.shape[0]
    return pl.pallas_call(
        functools.partial(last_kernel, n, rows_n),
        out_shape=jax.ShapeDtypeStruct((n, A_DEV * AW), jnp.bfloat16),
        in_specs=[smem(), vmem(), vmem(), vmem()] + [hbm() for _ in parts],
        out_specs=vmem(),
        scratch_shapes=[pltpu.VMEM(matrices(n), F32)] + own_scratch(parts),
        compiler_params=params(16),
        name="last",
    )(lax.axis_index(Z)[None], mirrored, r, l, *map(in_hbm, parts))


def on_device(rows_n, z_n, amplitudes, integrals, blocks):
    picked = gather(amplitudes, blocks, z_n)
    n = picked.shape[0] // (2 * z_n)
    parts, kept, sent, r, l = product(picked, integrals, z_n, (n, n // 2, n // 2))
    got = lax.ppermute(sent, XL, [(0, 1), (1, 0)])
    r, l = ring([parts], r, l, n)
    pieces = turn(r, l, parts, n, rows_n)
    shape = pieces.shape
    pieces = pieces.reshape((rows_n * 2,) + shape[2:])
    pieces = lax.all_to_all(pieces, (ROW, XL), 0, 0, tiled=True).reshape(shape)

    terms = [kept, got]
    r, l = ring(terms, *open_ring(terms, n // 2), n // 2)
    return last(pieces, r, l, terms, n // 2)


def solution(mesh):
    rows_n, cols_n = mesh.devices.shape
    finer = Mesh(mesh.devices.reshape(rows_n, cols_n // 2, 2), (ROW, Z, XL))
    return jax.shard_map(
        functools.partial(on_device, rows_n, cols_n // 2),
        mesh=finer,
        in_specs=(P(None, None, (Z, XL)), P((Z, XL), ROW), P()),
        out_specs=P((Z, XL), ROW),
        check_vma=False,
    )
```

```python
import functools

import jax
import jax.numpy as jnp
from jax import lax
from jax.experimental import pallas as pl
from jax.experimental.pallas import tpu as pltpu
from jax.sharding import Mesh
from jax.sharding import PartitionSpec as P

OB = 2
PB = OB * OB
A_DEV = 32
AW = 512
F32, I16 = jnp.float32, jnp.int16
ROW, Z, XL = "row", "z", "xl"
LANES = 128
TILES = A_DEV * AW // (16 * LANES)
ROW_W = TILES * LANES
PITCH = A_DEV + 1
TOP = 32700.0
STEPS = 256.0


def params(mib=32):
    return pltpu.CompilerParams(vmem_limit_bytes=mib << 20)


def cost(flops, bytes_accessed):
    return pl.CostEstimate(flops=flops, bytes_accessed=bytes_accessed, transcendentals=0)


def hbm():
    return pl.BlockSpec(memory_space=pltpu.HBM)


def vmem():
    return pl.BlockSpec(memory_space=pltpu.VMEM)


def scale_of(tiles):
    most = functools.reduce(jnp.maximum, [jnp.abs(t) for t in tiles])
    most = jnp.max(most, axis=0, keepdims=True)
    code = jnp.ceil(jnp.log2(jnp.maximum(most, 2.0**-100)) * STEPS)
    return code, TOP * jnp.exp2(code * (-1.0 / STEPS))


def coded(x, factor):
    return jnp.round(x * factor).astype(jnp.int32).astype(I16)


def factors(codes):
    return jnp.exp2(codes.astype(F32) * (1.0 / STEPS)) * (1.0 / TOP)


def column(k, n):
    return k * ROW_W + (LANES if k >= n // 2 else 0)


def get_row(ref, start, factor):
    return [
        ref[:, start + t * LANES : start + (t + 1) * LANES].astype(jnp.int32).astype(F32) * factor
        for t in range(TILES)
    ]


def put_row(ref, start, tiles):
    code, factor = scale_of(tiles)
    for t, tile in enumerate(tiles):
        ref[:, start + t * LANES : start + (t + 1) * LANES] = coded(tile, factor)
    return code


def scale_tile(codes):
    rows = codes + [jnp.zeros((1, LANES), F32)] * (16 - len(codes))
    return jnp.concatenate(rows, axis=0).astype(jnp.int32).astype(I16)


UNROLL = 4


def gather_kernel(z_n, at, blocks, pages, out, picked):
    depth, orbitals = pages.shape[1], pages.shape[2]
    pairs = blocks.shape[1]
    each = pairs // (2 * z_n)
    lane = lax.broadcasted_iota(jnp.int32, (depth, LANES), 1)
    blank = jnp.zeros((depth, LANES - orbitals), F32)
    picked[...] = jnp.zeros_like(picked)

    def turned(page, shift):
        whole = jnp.concatenate([pages[page].astype(F32), blank], axis=1)
        return pltpu.roll(whole, lax.rem(shift + LANES, LANES), 1)

    def some(step, _):
        forward, mirrored = picked[0], picked[1]
        for i in range(UNROLL):
            pair = step * UNROLL + i
            first, second = blocks[0, pair] * OB, blocks[1, pair] * OB
            device, g = pair // each, lax.rem(pair, each)
            z, other = device // 2, lax.rem(device + at[0], 2)
            base_f = (other * z_n + z) * each * PB + g * PB
            for s in range(OB):
                to = base_f + s * OB
                here = (lane >= to) & (lane < to + OB)
                forward = jnp.where(here, turned(first + s, to - second), forward)
                to = pair * PB + s * OB
                here = (lane >= to) & (lane < to + OB)
                mirrored = jnp.where(here, turned(second + s, to - first), mirrored)
        picked[0] = forward
        picked[1] = mirrored
        return 0

    lax.fori_loop(0, pairs // UNROLL, some, 0)
    mirrored = picked[1]
    which = lax.rem(lane, PB)
    mirrored = jnp.where(
        which == 1, pltpu.roll(mirrored, LANES - 1, 1), jnp.where(which == 2, pltpu.roll(mirrored, 1, 1), mirrored)
    )
    out[:LANES] = mirrored.T.astype(out.dtype)
    out[LANES:] = picked[0].T.astype(out.dtype)


def gather(amplitudes, blocks, z_n):
    depth = amplitudes.shape[2]
    rows = blocks.shape[0] * PB
    return pl.pallas_call(
        functools.partial(gather_kernel, z_n),
        out_shape=jax.ShapeDtypeStruct((2 * rows, depth), jnp.bfloat16),
        in_specs=[smem(), smem(), vmem()],
        out_specs=vmem(),
        scratch_shapes=[pltpu.VMEM((2, depth, LANES), F32)],
        compiler_params=params(24),
        name="pick_rows",
    )(lax.axis_index(XL)[None], blocks.T, jnp.swapaxes(amplitudes, 1, 2))


GRID = 4


def fill(left, right, whole):
    step = pl.program_id(0)
    rows = left.shape[0]
    each = A_DEV // GRID
    for i in range(each):
        part = jnp.dot(left[...], right[:, i * AW : (i + 1) * AW], preferred_element_type=F32)
        for c in range(AW // LANES):
            whole[c, pl.ds(step * each + i, rows, stride=PITCH), :] = part[:, c * LANES : (c + 1) * LANES]


def filled(whole, row):
    return [
        whole[c, pl.ds(row * PITCH + h * 16, 16), :] for h in range(2) for c in range(AW // LANES)
    ]


def product_kernel(segments, at, left, right, *refs):
    count = len(segments)
    parts, (out_r, out_l, whole) = refs[:count], refs[count : count + 3]
    coded_rows, sems = refs[count + 3 : 2 * count + 3], refs[-1]
    fill(left, right, whole)

    @pl.when(pl.program_id(0) == GRID - 1)
    def _():
        z_n = parts[0].shape[0]
        first_row = 0
        for i, n in enumerate(segments):
            middle = n // 2 * ROW_W

            def one(z, _, i=i, n=n, first_row=first_row, middle=middle):
                spot = coded_rows[i].at[z]
                codes = [put_row(spot, column(k, n), filled(whole, first_row + z * n + k)) for k in range(n)]
                spot[:, middle : middle + LANES] = scale_tile(codes)
                pltpu.make_async_copy(spot, parts[i].at[z], sems.at[i, z]).start()
                return 0

            lax.fori_loop(0, z_n, one, 0)
            if i == 0:
                opposite = coded_rows[0].at[at[0]]
                out_r[...] = opposite[:, : middle + LANES]
                out_l[...] = opposite[:, middle:]
            first_row += z_n * n
        for i in range(count):
            for z in range(z_n):
                pltpu.make_async_copy(coded_rows[i].at[z], parts[i].at[z], sems.at[i, z]).wait()


def far_side(z_n):
    return lax.rem(lax.axis_index(Z) + z_n // 2, z_n)[None]


def product(left, integrals, z_n, segments):
    rows, depth = left.shape
    width = integrals.shape[1]
    end = jax.ShapeDtypeStruct((16, segments[0] // 2 * ROW_W + LANES), I16)
    shapes = [(z_n, 16, n * ROW_W + LANES) for n in segments]
    return pl.pallas_call(
        functools.partial(product_kernel, segments),
        grid=(GRID,),
        out_shape=[pltpu.HBM(shape, I16) for shape in shapes] + [end, end],
        in_specs=[
            smem(),
            pl.BlockSpec((rows, depth), lambda s: (0, 0)),
            pl.BlockSpec((depth, width // GRID), lambda s: (0, s)),
        ],
        out_specs=[hbm() for _ in shapes] + [pl.BlockSpec(end.shape, lambda s: (0, 0))] * 2,
        scratch_shapes=[pltpu.VMEM(matrices(rows), F32)]
        + [pltpu.VMEM(shape, I16) for shape in shapes]
        + [pltpu.SemaphoreType.DMA((len(segments), z_n))],
        compiler_params=params(48),
        cost_estimate=cost(2 * rows * depth * width, 2 * depth * width + 2 * rows * width),
        name="product",
    )(far_side(z_n), left, in_hbm(integrals))


def in_hbm(x):
    return pltpu.with_memory_space_constraint(x, pltpu.HBM)


def matrices(rows):
    return (AW // LANES, rows * PITCH, LANES)


def smem():
    return pl.BlockSpec(memory_space=pltpu.SMEM)


def anywhere():
    return pl.BlockSpec(memory_space=pl.ANY)


def scales(ref, n):
    middle = n // 2 * ROW_W
    return factors(ref[:, middle : middle + LANES].astype(jnp.int32))


def total_row(refs, scale, k, n):
    rows = [get_row(ref, column(k, n), f[k : k + 1]) for ref, f in zip(refs, scale)]
    return [functools.reduce(jnp.add, tiles) for tiles in zip(*rows)]


def fetch(parts, at, own, sems):
    copies = [pltpu.make_async_copy(part.at[at], own.at[i], sems.at[i]) for i, part in enumerate(parts)]
    for copy in copies:
        copy.start()

    def wait():
        for copy in copies:
            copy.wait()

    return wait


def own_scratch(parts):
    return [pltpu.VMEM((len(parts),) + parts[0].shape[1:], I16), pltpu.SemaphoreType.DMA((len(parts),))]


def open_kernel(n, at, *refs):
    *parts, out_r, out_l, own, sems = refs
    fetch(parts, at[0], own, sems)()
    terms = [own.at[i] for i in range(len(parts))]
    f = [scales(ref, n) for ref in terms]
    half = n // 2
    for out, rows in ((out_r, range(half)), (out_l, range(half, n))):
        start = 0 if out is out_r else LANES
        codes = [jnp.zeros((1, LANES), F32)] * rows[0]
        for i, k in enumerate(rows):
            codes.append(put_row(out, start + i * ROW_W, total_row(terms, f, k, n)))
        spot = half * ROW_W if out is out_r else 0
        out[:, spot : spot + LANES] = scale_tile(codes)


def open_ring(parts, n):
    z_n = parts[0].shape[0]
    end = jax.ShapeDtypeStruct((16, n // 2 * ROW_W + LANES), I16)
    return pl.pallas_call(
        functools.partial(open_kernel, n),
        out_shape=[end, end],
        in_specs=[smem()] + [hbm() for _ in parts],
        out_specs=[vmem(), vmem()],
        scratch_shapes=own_scratch(parts),
        compiler_params=params(16),
        cost_estimate=cost(1000, 3000000),
        name="open_ring",
    )(far_side(z_n), *map(in_hbm, parts))


def step_kernel(n, side, first, at, got, *refs):
    *parts, _, out, own, sems = refs
    half = n // 2
    middle = half * ROW_W
    wait = fetch(parts, at[0], own, sems)
    spot = (middle if side == 0 else 0) if first else middle
    got_f = factors(got[:, spot : spot + LANES].astype(jnp.int32))
    wait()
    terms = [own.at[i] for i in range(len(parts))]
    f = [scales(ref, n) for ref in terms]
    codes = []
    for k in range(n):
        start = column(k, n)
        tiles = total_row(terms, f, k, n)
        if not first or (k < half) == (side == 0):
            came = get_row(got, start - (middle if first and side == 1 else 0), got_f[k : k + 1])
            tiles = [a + b for a, b in zip(tiles, came)]
        codes.append(put_row(out, start, tiles))
    out[:, middle : middle + LANES] = scale_tile(codes)


def ring_step(got, parts, at, n, side, first, after):
    width = parts[0].shape[2]
    return pl.pallas_call(
        functools.partial(step_kernel, n, side, first),
        out_shape=jax.ShapeDtypeStruct((16, width), I16),
        in_specs=[smem(), vmem()] + [hbm() for _ in parts] + [anywhere()],
        out_specs=vmem(),
        scratch_shapes=own_scratch(parts),
        compiler_params=params(16),
        cost_estimate=cost(1000, 3000000),
        name="ring_step",
    )(at, got, *map(in_hbm, parts), after)


def ring(parts, r, l, n):
    z_n = parts[0].shape[0]
    me = lax.axis_index(Z)
    right = [(i, (i + 1) % z_n) for i in range(z_n)]
    left = [((i + 1) % z_n, i) for i in range(z_n)]
    far = z_n // 2
    r, l = lax.ppermute(r, Z, right), lax.ppermute(l, Z, left)
    for d in range(far - 1, 0, -1):
        first = d == far - 1
        at = lax.rem(me + d, z_n)[None]
        r = ring_step(r, parts, at, n, 0, first, at)
        l = ring_step(l, parts, lax.rem(me + z_n - d, z_n)[None], n, 1, first, r)
        r, l = lax.ppermute(r, Z, right), lax.ppermute(l, Z, left)
    return r, l


def matrix(tiles):
    per = len(tiles) // 2
    return jnp.concatenate(
        [jnp.concatenate(tiles[:per], axis=1), jnp.concatenate(tiles[per:], axis=1)], axis=0
    )


def turn_kernel(n, rows_n, at, got_r, got_l, parts, out, own, sems):
    fetch([parts], at[0], own, sems)()
    terms = [got_r, got_l, own.at[0]]
    f = [scales(ref, n) for ref in terms]
    groups = n // (2 * PB)
    for xl in range(2):
        codes = []
        for g in range(groups):
            stack = jnp.concatenate([matrix(total_row(terms, f, (xl * groups + g) * PB + i, n)) for i in range(PB)], axis=0)
            turned = stack.T
            code, factor = scale_of([turned])
            codes.append(code)
            for to in range(rows_n):
                out[to, xl, g * A_DEV : (g + 1) * A_DEV, :] = coded(turned[to * A_DEV : (to + 1) * A_DEV], factor)
        tile = scale_tile(codes)
        for to in range(rows_n):
            out[to, xl, groups * A_DEV : groups * A_DEV + 16, :] = tile


def turn(got_r, got_l, parts, n, rows_n):
    width = parts.shape[2]
    shape = (rows_n, 2, n // (2 * PB) * A_DEV + 16, LANES)
    return pl.pallas_call(
        functools.partial(turn_kernel, n, rows_n),
        out_shape=jax.ShapeDtypeStruct(shape, I16),
        in_specs=[smem(), vmem(), vmem(), hbm()],
        out_specs=vmem(),
        scratch_shapes=own_scratch([parts]),
        compiler_params=params(32),
        cost_estimate=cost(16 * width * 8, 16 * width * 8),
        name="turn",
    )(lax.axis_index(Z)[None], got_r, got_l, in_hbm(parts))


def regroup(tiles):
    count = len(tiles)
    group = LANES // count
    lane = lax.broadcasted_iota(jnp.int32, tiles[0].shape, 1) // group
    out = []
    for k in range(count):
        merged = tiles[k]
        for r in range(count):
            if r != k:
                merged = jnp.where(lane == r, pltpu.roll(tiles[r], (r - k) % count * group, 1), merged)
        out.append(merged)
    return out


def last_kernel(n, rows_n, at, mirrored, r, l, *refs):
    *parts, out, total, own, sems = refs
    wait = fetch(parts, at[0], own, sems)
    groups = n // PB
    spot = groups * A_DEV
    f = [[factors(mirrored[row, s, spot : spot + 16, :].astype(jnp.int32)) for s in range(2)] for row in range(rows_n)]
    for g in range(groups):
        pieces = []
        for row in range(rows_n):
            both = [
                mirrored[row, s, g * A_DEV : (g + 1) * A_DEV, :].astype(jnp.int32).astype(F32) * f[row][s][g : g + 1]
                for s in range(2)
            ]
            pieces.append(both[0] + both[1])
        per = LANES // A_DEV
        for c in range(rows_n // per):
            for i, tile in enumerate(regroup(pieces[c * per : (c + 1) * per])):
                total[c, pl.ds((g * PB + i) * PITCH, A_DEV), :] = tile
    wait()
    terms = [r, l] + [own.at[i] for i in range(len(parts))]
    scale = [scales(ref, n) for ref in terms]
    for k in range(n):
        tiles = total_row(terms, scale, k, n)
        for h in range(2):
            for c in range(AW // LANES):
                total[c, pl.ds(k * PITCH + h * 16, 16), :] += tiles[h * (AW // LANES) + c]
    for a in range(A_DEV):
        for c in range(AW // LANES):
            start = a * AW + c * LANES
            out[:, start : start + LANES] = total[c, pl.ds(a, n, stride=PITCH), :].astype(out.dtype)


def last(mirrored, r, l, parts, n):
    rows_n = mirrored.shape[0]
    return pl.pallas_call(
        functools.partial(last_kernel, n, rows_n),
        out_shape=jax.ShapeDtypeStruct((n, A_DEV * AW), jnp.bfloat16),
        in_specs=[smem(), vmem(), vmem(), vmem()] + [hbm() for _ in parts],
        out_specs=vmem(),
        scratch_shapes=[pltpu.VMEM(matrices(n), F32)] + own_scratch(parts),
        compiler_params=params(16),
        name="last",
    )(lax.axis_index(Z)[None], mirrored, r, l, *map(in_hbm, parts))


def on_device(rows_n, z_n, amplitudes, integrals, blocks):
    picked = gather(amplitudes, blocks, z_n)
    n = picked.shape[0] // (2 * z_n)
    parts, kept, sent, r, l = product(picked, integrals, z_n, (n, n // 2, n // 2))
    got = lax.ppermute(sent, XL, [(0, 1), (1, 0)])
    r, l = ring([parts], r, l, n)
    pieces = turn(r, l, parts, n, rows_n)
    shape = pieces.shape
    pieces = pieces.reshape((rows_n * 2,) + shape[2:])
    pieces = lax.all_to_all(pieces, (ROW, XL), 0, 0, tiled=True).reshape(shape)

    terms = [kept, got]
    r, l = ring(terms, *open_ring(terms, n // 2), n // 2)
    return last(pieces, r, l, terms, n // 2)


def solution(mesh):
    rows_n, cols_n = mesh.devices.shape
    finer = Mesh(mesh.devices.reshape(rows_n, cols_n // 2, 2), (ROW, Z, XL))
    return jax.shard_map(
        functools.partial(on_device, rows_n, cols_n // 2),
        mesh=finer,
        in_specs=(P(None, None, (Z, XL)), P((Z, XL), ROW), P()),
        out_specs=P((Z, XL), ROW),
        check_vma=False,
    )
```
